256 devices in a mesh: row: 8 (over y, x_lo), col: 16 (over z, core), frame: 2 (over x_hi).
Axes of the slice: x: 4 (x_hi: 2, x_lo: 2; x = x_hi * 2 + x_lo), y: 4, z: 8, core: 2. Of those that a mesh axis runs over, the one named last changes fastest.
Arguments:
- tokens: bfloat16 [131072, 1536], P(('frame', 'row', 'col')), parts along dimension 0, may hold values from -6 to 6
- project_weight: bfloat16 [1536, 384], replicated, may hold values from -0.15625 to 0.15625
- project_bias: float32 [384], replicated, may hold values from -3 to 3
- inner_weight: bfloat16 [3, 3, 384, 384], replicated, may hold values from -0.109375 to 0.109375
- inner_bias: float32 [384], replicated, may hold values from -3 to 3
- outer_weight: bfloat16 [3, 3, 384, 384], replicated, may hold values from -0.109375 to 0.109375
- outer_bias: float32 [384], replicated, may hold values from -3 to 3
- cotangent: bfloat16 [512, 256, 384], P(('frame', 'row'), 'col'), parts along dimension 0, may hold values from -6 to 6
Outputs:
- refined: bfloat16 [512, 256, 384], P(('frame', 'row'), 'col'), parts along dimension 0
- grad_tokens: bfloat16 [131072, 1536], P(('frame', 'row', 'col')), parts along dimension 0
- grad_project: float32 [3072, 384], P(('frame', 'row'), 'col'), parts along dimension 0
- grad_inner: float32 [6, 3, 384, 384], P('frame', None, 'row', 'col'), parts along dimension 0
- grad_outer: float32 [6, 3, 384, 384], P('frame', None, 'row', 'col'), parts along dimension 0
The draws below stay inside these ranges and needn't reach their ends.
There are 2 independent parts, one for each index of `frame`. The reference program is written for one: setup_inputs(seed, part) draws one part's arguments, and reference() takes and returns one part's arrays. A program takes and returns all parts, laid end to end along the dimension named above; an argument that names none is the same for every part. Nothing has to cross between parts.
All inputs are finite; a program needn't handle non-finite values.
Results may differ from the reference program's by a relative error of at most 0.027.
Values may be sent and summed in bfloat16 or wider, within the bound.
A program may use at most 128 MiB of HBM per device.

```python
import math
import jax
import jax.numpy as jnp
from jax import lax

VIT_DIM = 1536
JOIN_DIM = 384
GRID_ROWS = 256
GRID_COLS = 256
TOKENS = 65536


def shard_levels(rng, dims, cuts, low, top_value):
    factor_of, own = 1.0, jax.random.fold_in(rng, 6)
    for axis_at, parts in cuts:
        steps = jnp.exp(jax.random.uniform(jax.random.fold_in(own, axis_at), (parts,), jnp.float32, low / len(cuts), top_value / len(cuts)))
        factor_of = factor_of * jnp.repeat(steps, dims[axis_at] // parts).reshape([-1 if axis == axis_at else 1 for axis in range(len(dims))])
    return factor_of


def scatter_about(stream_key, shape, scale, bound, split=(), held_as=jnp.bfloat16):
    array = scale * jax.random.normal(stream_key, shape, jnp.float32)
    if split:
        array = array * shard_levels(stream_key, shape, split, -0.22, 0.18)
    return jnp.clip(array, -bound, bound).astype(held_as)


def setup_inputs(seed: int = 0, part: int = 0) -> dict:
    streams_of = jax.random.split(jax.random.key(seed), 9)
    own_keys = jax.random.split(jax.random.fold_in(streams_of[8], part), 9)
    return {
        "tokens": scatter_about(own_keys[0], (TOKENS, VIT_DIM), 1.0, 6.0, ((0, 128),)),
        "project_weight": scatter_about(streams_of[1], (VIT_DIM, JOIN_DIM), VIT_DIM ** -0.5, 0.15625),
        "project_bias": scatter_about(streams_of[2], (JOIN_DIM,), 0.5, 3.0, (), jnp.float32),
        "inner_weight": scatter_about(streams_of[3], (3, 3, JOIN_DIM, JOIN_DIM), (9 * JOIN_DIM) ** -0.5, 0.109375),
        "inner_bias": scatter_about(streams_of[4], (JOIN_DIM,), 0.5, 3.0, (), jnp.float32),
        "outer_weight": scatter_about(streams_of[5], (3, 3, JOIN_DIM, JOIN_DIM), (9 * JOIN_DIM) ** -0.5, 0.109375),
        "outer_bias": scatter_about(streams_of[6], (JOIN_DIM,), 0.5, 3.0, (), jnp.float32),
        "cotangent": scatter_about(own_keys[7], (GRID_ROWS, GRID_COLS, JOIN_DIM), 1.0, 6.0, ((0, 8), (1, 16))),
    }


def silu_slope(value):
    sigma = jax.nn.sigmoid(value)
    return sigma * (1.0 + value * (1.0 - sigma))

def zero_rim(field):
    return jnp.pad(field, ((1, 1), (1, 1), (0, 0)))

def conv_apply(padded, kernel):
    rows_here = padded.shape[0] - 2
    cols_here = padded.shape[1] - 2
    chans = padded.shape[2]
    total = jnp.zeros((rows_here * cols_here, kernel.shape[3]), jnp.float32)
    for top in range(3):
        for left in range(3):
            window = padded[top:top + rows_here, left:left + cols_here].reshape(rows_here * cols_here, chans)
            total = total + jnp.dot(window, kernel[top, left], preferred_element_type=jnp.float32)
    return total.reshape(rows_here, cols_here, kernel.shape[3])

def conv_transpose(padded, kernel):
    rows_here = padded.shape[0] - 2
    cols_here = padded.shape[1] - 2
    chans = padded.shape[2]
    total = jnp.zeros((rows_here * cols_here, kernel.shape[2]), jnp.float32)
    for top in range(3):
        for left in range(3):
            window = padded[2 - top:2 - top + rows_here, 2 - left:2 - left + cols_here].reshape(rows_here * cols_here, chans)
            total = total + jnp.dot(window, kernel[top, left].T, preferred_element_type=jnp.float32)
    return total.reshape(rows_here, cols_here, kernel.shape[2])

def weight_grad(padded, upstream):
    rows_here = upstream.shape[0]
    cols_here = upstream.shape[1]
    chans = padded.shape[2]
    flat_up = upstream.reshape(rows_here * cols_here, upstream.shape[2])
    blocks = []
    for top in range(3):
        for left in range(3):
            window = padded[top:top + rows_here, left:left + cols_here].reshape(rows_here * cols_here, chans)
            blocks.append(lax.dot_general(window, flat_up, (((0,), (0,)), ((), ())), preferred_element_type=jnp.float32))
    return jnp.stack(blocks).reshape(3, 3, chans, upstream.shape[2])

def refine(feature, cotangent, inner_weight, inner_bias, outer_weight, outer_bias, margin):
    feature_wide = feature.astype(jnp.float32)
    activated = jax.nn.silu(feature_wide).astype(jnp.bfloat16)
    activated_rim = margin(activated)
    pre_hidden = conv_apply(activated_rim, inner_weight) + inner_bias
    hidden = jax.nn.silu(pre_hidden).astype(jnp.bfloat16)
    hidden_rim = margin(hidden)
    refined = (feature_wide + conv_apply(hidden_rim, outer_weight) + outer_bias).astype(jnp.bfloat16)
    grad_outer = weight_grad(hidden_rim, cotangent)
    back_hidden = (conv_transpose(margin(cotangent), outer_weight) * silu_slope(pre_hidden)).astype(jnp.bfloat16)
    grad_inner = weight_grad(activated_rim, back_hidden)
    back_feature = (cotangent.astype(jnp.float32) + conv_transpose(margin(back_hidden), inner_weight) * silu_slope(feature_wide)).astype(jnp.bfloat16)
    return (refined, back_feature, grad_inner, grad_outer)

def reference(tokens, project_weight, project_bias, inner_weight, inner_bias, outer_weight, outer_bias, cotangent):
    scale = 1.0 / math.sqrt(GRID_ROWS * GRID_COLS)
    feature = (jnp.dot(tokens, project_weight, preferred_element_type=jnp.float32) + project_bias).astype(jnp.bfloat16)
    feature = feature.reshape(GRID_ROWS, GRID_COLS, JOIN_DIM)
    refined, back_feature, grad_inner, grad_outer = refine(feature, cotangent, inner_weight, inner_bias, outer_weight, outer_bias, zero_rim)
    flat_back = back_feature.reshape(TOKENS, JOIN_DIM)
    grad_project = lax.dot_general(tokens, flat_back, (((0,), (0,)), ((), ())), preferred_element_type=jnp.float32)
    grad_tokens = jnp.dot(flat_back, project_weight.T, preferred_element_type=jnp.float32).astype(jnp.bfloat16)
    return (refined, grad_tokens, grad_project * scale, grad_inner * scale, grad_outer * scale)
```

```python
import math

import jax
import jax.numpy as jnp
from jax import lax
from jax.experimental import pallas as pl
from jax.experimental.pallas import tpu as pltpu
from jax.sharding import PartitionSpec as P

VIT = 1536
DIM = 384
WIDE = 3 * DIM
COLS = 256
TOK = 512
TILE_ROWS = 32
TILE_COLS = 16
NY = 4
NX = 2
NZ = 8
NCOL = 16
NROW = 8
BF = jnp.bfloat16
F32 = jnp.float32
MESH = pl.DeviceIdType.MESH

ROW_PIECES = (
    ("o1", 96, 48, (3, 4, 5)),
    ("o2", 144, 144, (0, 1, 2, 6, 7, 8)),
    ("i1", 48, 96, (3, 4, 5)),
    ("i2", 144, 144, (0, 1, 2, 6, 7, 8)),
    ("p", 96, 96, ()),
)
Z_PIECES = (("zo", 256), ("zi", 256), ("zp", 128))
CORE, XAX, YAX, NROWSEM = 0, 1, 2, 8
SWAP, NZSEM = 7, 8


def scratch_table():
    table = {
        "tok": ((TOK, VIT), BF),
        "tok_t": ((VIT, TOK), BF),
        "wp": ((VIT, DIM), BF),
        "wi": ((3, WIDE, DIM), BF),
        "wo": ((3, WIDE, DIM), BF),
        "act": ((4, COLS, DIM), BF),
        "hid": ((4, COLS, DIM), BF),
        "cot": ((4, COLS, DIM), BF),
        "bh": ((4, COLS, DIM), BF),
        "ea": ((4 * COLS, WIDE), BF),
        "eh": ((4 * COLS, WIDE), BF),
        "ec": ((4 * COLS, WIDE), BF),
        "feat": ((TOK, DIM), BF),
        "bf": ((TOK, DIM), BF),
        "slope": ((TOK, DIM), F32),
        "act_t": ((DIM, TOK), BF),
        "hid_t": ((DIM, TOK), BF),
        "strip": ((2, COLS, DIM), BF),
        "tile": ((TILE_ROWS, TILE_COLS, DIM), BF),
        "gtok": ((TOK, VIT), BF),
    }
    for name, n0, n1, _ in ROW_PIECES:
        nm = max(n0, n1)
        table |= {
            name + "_part": ((NROW, n0 + n1, DIM), BF),
            name + "_core": ((NROW, nm, DIM), BF),
            name + "_sum": ((NY, NX, nm, DIM), BF),
            name + "_xr": ((NY, nm, DIM), BF),
            name + "_sx": ((NY, nm, DIM), BF),
            name + "_yr": ((6, nm, DIM), BF),
            name + "_fw": ((2, nm, DIM), BF),
        }
    for name, lanes in Z_PIECES:
        table |= {
            name + "_red": ((lanes, DIM), F32),
            name + "_zs": ((NZ, DIM // NZ, lanes), BF),
            name + "_zr": ((NZ - 1, DIM // NZ, lanes), BF),
            name + "_fs": ((2, DIM // NCOL, lanes), F32),
            name + "_fr": ((DIM // NCOL, lanes), F32),
        }
    out = {k: pltpu.VMEM(*v) for k, v in table.items()}
    for group, count in ((ROW_PIECES, NROWSEM), (Z_PIECES, NZSEM)):
        for piece in group:
            out[piece[0] + "_ss"] = pltpu.SemaphoreType.DMA((count,))
            out[piece[0] + "_rs"] = pltpu.SemaphoreType.DMA((count,))
    out["load"] = pltpu.SemaphoreType.DMA((10,))
    out["halo_ss"] = pltpu.SemaphoreType.DMA((8,))
    out["halo_rs"] = pltpu.SemaphoreType.DMA((8,))
    out["swap_ss"] = pltpu.SemaphoreType.DMA((30,))
    out["swap_rs"] = pltpu.SemaphoreType.DMA((30,))
    return out


def dot(a, b):
    return jnp.dot(a, b, preferred_element_type=F32)


def dot_nt(a, b):
    return lax.dot_general(a, b, (((1,), (1,)), ((), ())), preferred_element_type=F32)


def silu(v):
    return v * jax.nn.sigmoid(v)


def silu_slope(v):
    s = jax.nn.sigmoid(v)
    return s * (1.0 + v * (1.0 - s))


class Where:
    def __init__(self):
        self.r = lax.axis_index("row")
        self.c = lax.axis_index("col")
        self.y = self.r // 2
        self.x = self.r % 2
        self.z = self.c // 2
        self.core = self.c % 2
        here = self.r * NCOL + self.c
        above = (here + NROW * NCOL - 1) % (NROW * NCOL)
        below = (here + 1) % (NROW * NCOL)
        self.up = {"row": above // NCOL, "col": above % NCOL}
        self.down = {"row": below // NCOL, "col": below % NCOL}
        self.first = here == 0
        self.last = here == NROW * NCOL - 1
        self.pair = {"col": self.z * 2 + 1 - self.core}
        self.across = {"row": self.y * 2 + 1 - self.x}

    def at_y(self, k):
        return {"row": ((self.y + k) % NY) * 2 + self.x}

    def at_z(self, k):
        return {"col": ((self.z + k) % NZ) * 2 + self.core}

    def at_col(self, k):
        return {"col": (self.c + k) % NCOL}


def remote(src, dst, ss, rs, device):
    return pltpu.make_async_remote_copy(
        src_ref=src, dst_ref=dst, send_sem=ss, recv_sem=rs, device_id=device, device_id_type=MESH
    )


def per_core(w, step):
    for k in (0, 1):
        pl.when(w.core == k)(lambda k=k: step(k))


class RowPiece:
    def __init__(self, w, m, name, n0, n1, red, at):
        self.w = w
        self.n = (n0, n1)
        self.off = (0, n0)
        self.out = (red, at)
        for field in ("part", "core", "sum", "xr", "sx", "yr", "fw", "ss", "rs"):
            setattr(self, field, m[name + "_" + field])

    def copy(self, src, dst, k, device):
        return remote(src, dst, self.ss.at[k], self.rs.at[k], device)

    def core_out(self, k):
        o, m = self.off[1 - k], self.n[1 - k]
        return self.copy(self.part.at[:, o : o + m], self.core.at[:, :m], CORE, self.w.pair)

    def core_in(self, k):
        n = self.n[k]
        return self.copy(self.core.at[:, :n], self.core.at[:, :n], CORE, self.w.pair)

    def stage0(self):
        per_core(self.w, lambda k: self.core_out(k).start())

    def x_copy(self, k):
        n = self.n[k]
        if k == 0:
            src, dst = self.sum.at[:, 1 - self.w.x, :n], self.xr.at[:, :n]
        else:
            src, dst = self.sx.at[1 - self.w.x, :n], self.xr.at[0, :n]
        return self.copy(src, dst, XAX, self.w.across)

    def halves(self, k):
        n = self.n[k]
        if k == 1:
            return (pl.ds(0, n), pl.ds(0, n))
        low = (n // 32) * 16
        return (pl.ds(0, low), pl.ds(low, n - low))

    def block(self, k, t, h):
        if k == 1:
            return self.sum.at[t, h, pl.ds(0, self.n[1])]
        return self.sx.at[t, self.halves(0)[h]]

    def slot(self, k, s, h):
        return self.yr.at[s, pl.ds(0, self.halves(k)[h].size)]

    def forward(self, k, h):
        return self.fw.at[h, pl.ds(0, self.halves(k)[h].size)]

    def y_copy(self, k, j):
        w = self.w
        far, before, after = (w.y + 2) % NY, (w.y + 3) % NY, (w.y + 1) % NY
        h = j % 2
        step = (1, 3, 3, 1, 1, 3)[j]
        if j < 4:
            src = self.block(k, (far, far, before, after)[j], h)
        else:
            src = self.forward(k, h)
        return self.copy(src, self.slot(k, j, h), YAX + j, w.at_y(step))

    def y_first(self, k):
        for j in range(4):
            self.y_copy(k, j).start()

    def y_second(self, k):
        for h, t in ((0, (self.w.y + 1) % NY), (1, (self.w.y + 3) % NY)):
            self.y_copy(k, h).wait_recv()
            self.forward(k, h)[...] = self.block(k, t, h)[...] + self.slot(k, h, h)[...]
            self.y_copy(k, 4 + h).start()

    def y_end(self, k, h):
        self.y_copy(k, 2 + h).wait_recv()
        self.y_copy(k, 4 + h).wait_recv()
        return (
            self.block(k, self.w.y, h)[...].astype(F32)
            + self.slot(k, 4 + h, h)[...].astype(F32)
            + self.slot(k, 2 + h, h)[...].astype(F32)
        )

    def stage1(self):
        def step(k):
            n, o = self.n[k], self.off[k]
            self.core_in(k).wait_recv()
            for j in range(NROW):
                self.sum[j // NX, j % NX, :n] = self.part[j, o : o + n] + self.core[j, :n]
            if k == 0:
                self.x_copy(0).start()
            else:
                self.y_first(1)

        per_core(self.w, step)

    def stage2(self):
        def step(k):
            if k == 0:
                n = self.n[0]
                self.x_copy(0).wait_recv()
                for t in range(NY):
                    self.sx[t, :n] = self.sum[t, self.w.x, :n] + self.xr[t, :n]
                self.y_first(0)
            else:
                self.y_second(1)

        per_core(self.w, step)

    def stage3(self):
        def step(k):
            if k == 0:
                self.y_second(0)
            else:
                for h in (0, 1):
                    self.sx[h, : self.n[1]] = self.y_end(1, h).astype(BF)
                self.x_copy(1).start()

        per_core(self.w, step)

    def stage4(self):
        def step(k):
            red, at = self.out[0], self.out[1][k]
            n = self.n[k]
            if k == 0:
                for h in (0, 1):
                    rows = self.halves(0)[h]
                    red[at + rows.start : at + rows.start + rows.size] = self.y_end(0, h)
            else:
                self.x_copy(1).wait_recv()
                red[at : at + n] = self.sx[self.w.x, :n].astype(F32) + self.xr[0, :n].astype(F32)

        per_core(self.w, step)

    def finish(self):
        def step(k):
            self.core_out(k).wait_send()
            self.x_copy(k).wait_send()
            for j in range(6):
                self.y_copy(k, j).wait_send()

        per_core(self.w, step)


class ZPiece:
    def __init__(self, w, m, name, lanes, rows):
        self.w = w
        self.lanes = lanes
        self.rows = rows
        for field in ("red", "zs", "zr", "fs", "fr", "ss", "rs"):
            setattr(self, field, m[name + "_" + field])

    def copy(self, d):
        w = self.w
        if d == 0:
            src, dst, k, device = self.fs.at[1 - w.core], self.fr, SWAP, w.pair
        else:
            src, dst, k, device = self.zs.at[(w.z + d) % NZ], self.zr.at[d - 1], d - 1, w.at_z(d)
        return remote(src, dst, self.ss.at[k], self.rs.at[k], device)

    def clear(self):
        low = min(self.rows)
        self.red[low:] = jnp.zeros((self.lanes - low, DIM), F32)

    def stage4(self):
        self.zs[...] = self.red[...].T.astype(BF).reshape(NZ, DIM // NZ, self.lanes)
        for d in (4, 3, 5, 2, 6, 1, 7):
            self.copy(d).start()

    def stage5(self):
        total = self.zs[self.w.z].astype(F32)
        for d in range(1, NZ):
            self.copy(d).wait_recv()
            total = total + self.zr[d - 1].astype(F32)
        self.fs[...] = total.reshape(2, DIM // NCOL, self.lanes)
        self.copy(0).start()

    def stage6(self, put):
        self.copy(0).wait_recv()

        def step(k):
            put(k, self.fs[k])
            put(1 - k, self.fr[...])

        per_core(self.w, step)

    def finish(self):
        for d in range(NZ):
            self.copy(d).wait_send()


def kernel(names, scale, *refs):
    tok_h, wp_h, bp, wi_h, bi, wo_h, bo, cot_h = refs[:8]
    refined_o, gtok_o, gproj_o, gin_o, gout_o = refs[8:13]
    m = dict(zip(names, refs[13:]))
    w = Where()
    share, width = DIM // NCOL, DIM // NROW
    zo = ZPiece(w, m, "zo", 256, (240, 192))
    zi = ZPiece(w, m, "zi", 256, (192, 240))
    zp = ZPiece(w, m, "zp", 128, (96, 96))
    places = {"o1": (zo, (0, 0)), "o2": (zo, (96, 48)), "i1": (zi, (0, 0)), "i2": (zi, (48, 96)), "p": (zp, (0, 0))}
    rows, taps = {}, {}
    for name, n0, n1, taps[name] in ROW_PIECES:
        target, at = places[name]
        rows[name] = RowPiece(w, m, name, n0, n1, target.red, at)
    o1, o2, i1, i2, pp = rows.values()

    barrier = pltpu.get_barrier_semaphore()
    friends = [w.at_col(k) for k in range(1, NCOL)]
    friends += [w.across, w.at_y(1), w.at_y(3), w.up, w.down]
    for device in friends:
        pl.semaphore_signal(barrier, inc=1, device_id=device, device_id_type=MESH)

    load = m["load"]
    loads = [
        pltpu.make_async_copy(src, m[dst], load.at[k])
        for k, (src, dst) in enumerate(((tok_h, "tok"), (wp_h, "wp"), (wi_h, "wi"), (wo_h, "wo")))
    ]
    loads[0].start()
    loads[1].start()
    here = pl.ds(pl.multiple_of(w.c * TILE_COLS, TILE_COLS), TILE_COLS)
    mine = pl.ds(w.c * 2, 2)
    cot = m["cot"]

    def halo(center, k):
        up = remote(center.at[1], center.at[3], m["halo_ss"].at[k], m["halo_rs"].at[k], w.up)
        down = remote(center.at[2], center.at[0], m["halo_ss"].at[k + 1], m["halo_rs"].at[k + 1], w.down)
        up.start()
        down.start()
        return [down, up]

    keep_low = jnp.where(w.first, 0.0, 1.0).astype(F32)
    keep_high = jnp.where(w.last, 0.0, 1.0).astype(F32)

    def expand(center, wide, row, flip):
        v = center[row].astype(F32)
        if row == 0:
            v = v * keep_low
        if row == 3:
            v = v * keep_high
        at = lax.broadcasted_iota(jnp.int32, (COLS, DIM), 0)
        before = jnp.where(at == 0, 0.0, pltpu.roll(v, 1, 0))
        after = jnp.where(at == COLS - 1, 0.0, pltpu.roll(v, COLS - 1, 0))
        first, last = (after, before) if flip else (before, after)
        rows = pl.ds(row * COLS, COLS)
        wide[rows, 0:DIM] = first.astype(BF)
        wide[rows, DIM : 2 * DIM] = v.astype(BF)
        wide[rows, 2 * DIM : WIDE] = last.astype(BF)

    def expand_rim(center, wide, copies, flip):
        copies[0].wait_recv()
        expand(center, wide, 0, flip)
        copies[1].wait_recv()
        expand(center, wide, 3, flip)

    def conv(wide, kern):
        total = dot(wide[0:TOK], kern[0])
        total = total + dot(wide[COLS : COLS + TOK], kern[1])
        return total + dot(wide[2 * COLS : 2 * COLS + TOK], kern[2])

    def conv_t(wide, kern):
        total = jnp.zeros((TOK, DIM), F32)
        for a in range(3):
            at = slice((2 - a) * COLS, (2 - a) * COLS + TOK)
            for b in range(3):
                lanes = slice(b * DIM, (b + 1) * DIM)
                total = total + dot_nt(wide[at, lanes], kern[a, lanes])
        return total

    def weight_grad(left_t, wide, name):
        for a in sorted({t // 3 for t in taps[name]}):
            g = dot(left_t[...], wide[(2 - a) * COLS : (2 - a) * COLS + TOK])
            for b in range(3):
                at = taps[name].index(3 * a + b) * width
                rows[name].part[:, at : at + width] = (
                    g[:, b * DIM : (b + 1) * DIM].astype(BF).reshape(NROW, width, DIM)
                )

    act, hid, bh = m["act"], m["hid"], m["bh"]
    loads[0].wait()
    loads[1].wait()
    loads[2].start()
    own_cot = pltpu.make_async_copy(cot_h.at[mine], cot.at[pl.ds(1, 2), here], load.at[4])
    own_cot.start()
    feature = (dot(m["tok"][...], m["wp"][...]) + bp[...][None, :]).astype(BF)
    m["feat"][...] = feature
    activated = silu(feature.astype(F32)).astype(BF)
    act[1:3] = activated.reshape(2, COLS, DIM)

    pl.semaphore_wait(barrier, len(friends))

    act_halo = halo(act, 0)
    cot_copies = []
    for k in range(1, NCOL):
        there = (w.c + k) % NCOL
        cot_copies.append(
            remote(
                cot_h.at[pl.ds(there * 2, 2)],
                cot.at[pl.ds(1, 2), here],
                m["swap_ss"].at[k - 1],
                m["swap_rs"].at[k - 1],
                w.at_col(k),
            )
        )
        cot_copies[-1].start()
    loads[3].start()
    for z in (zo, zi, zp):
        z.clear()
    m["act_t"][...] = act[1:3].reshape(TOK, DIM).T
    expand(act, m["ea"], 1, False)
    expand(act, m["ea"], 2, False)
    m["tok_t"][...] = m["tok"][...].T
    expand_rim(act, m["ea"], act_halo, False)

    loads[2].wait()
    pre = conv(m["ea"], m["wi"]) + bi[...][None, :]
    hidden = silu(pre).astype(BF)
    m["slope"][...] = silu_slope(pre)
    hid[1:3] = hidden.reshape(2, COLS, DIM)
    hid_halo = halo(hid, 2)
    m["hid_t"][...] = hid[1:3].reshape(TOK, DIM).T
    expand(hid, m["eh"], 1, False)
    expand(hid, m["eh"], 2, False)

    own_cot.wait()
    for c in cot_copies:
        c.wait_recv()
    cot_halo = halo(cot, 4)
    expand(cot, m["ec"], 1, True)
    expand(cot, m["ec"], 2, True)
    weight_grad(m["hid_t"], m["ec"], "o1")
    o1.stage0()
    expand_rim(hid, m["eh"], hid_halo, False)
    loads[3].wait()
    refined = m["feat"][...].astype(F32) + conv(m["eh"], m["wo"]) + bo[...][None, :]
    m["strip"][...] = refined.astype(BF).reshape(2, COLS, DIM)
    o1.stage1()
    expand_rim(cot, m["ec"], cot_halo, True)

    bh[1:3] = (conv_t(m["ec"], m["wo"]) * m["slope"][...]).astype(BF).reshape(2, COLS, DIM)
    bh_halo = halo(bh, 6)
    weight_grad(m["hid_t"], m["ec"], "o2")
    o2.stage0()
    expand(bh, m["ea"], 1, True)
    expand(bh, m["ea"], 2, True)
    weight_grad(m["act_t"], m["ea"], "i1")
    i1.stage0()
    o1.stage2()
    o2.stage1()
    expand_rim(bh, m["ea"], bh_halo, True)

    own_refined = pltpu.make_async_copy(m["strip"].at[:, here], m["tile"].at[mine], load.at[5])
    own_refined.start()
    refined_copies = []
    for k in range(1, NCOL):
        there = (w.c + k) % NCOL
        refined_copies.append(
            remote(
                m["strip"].at[:, pl.ds(pl.multiple_of(there * TILE_COLS, TILE_COLS), TILE_COLS)],
                m["tile"].at[mine],
                m["swap_ss"].at[14 + k],
                m["swap_rs"].at[14 + k],
                w.at_col(k),
            )
        )
        refined_copies[-1].start()

    i1.stage1()
    weight_grad(m["act_t"], m["ea"], "i2")
    i2.stage0()
    o1.stage3()
    back = conv_t(m["ea"], m["wi"]) * silu_slope(m["feat"][...].astype(F32))
    back_feature = (cot[1:3].reshape(TOK, DIM).astype(F32) + back).astype(BF)
    m["bf"][...] = back_feature
    o2.stage2()
    i2.stage1()
    pp.part[...] = dot(m["tok_t"][...], m["bf"][...]).astype(BF).reshape(NROW, VIT // NROW, DIM)
    pp.stage0()
    i1.stage2()
    o1.stage4()
    o2.stage3()
    pp.stage1()
    i1.stage3()
    m["gtok"][...] = dot_nt(m["bf"][...], m["wp"][...]).astype(BF)
    gtok_copy = pltpu.make_async_copy(m["gtok"], gtok_o, load.at[6])
    gtok_copy.start()
    o2.stage4()
    zo.stage4()
    i2.stage2()
    i1.stage4()
    pp.stage2()
    i2.stage3()
    pp.stage3()
    i2.stage4()
    zi.stage4()
    pp.stage4()
    zp.stage4()
    zo.stage5()
    own_refined.wait()
    for c in refined_copies:
        c.wait_recv()
    refined_copy = pltpu.make_async_copy(m["tile"], refined_o, load.at[7])
    refined_copy.start()
    zi.stage5()
    zp.stage5()

    def put_taps(out, order):
        def put(k, value):
            for j, t in enumerate(order[k]):
                out[t] = value[:, j * width : (j + 1) * width] * scale

        return put

    def put_project(k, value):
        gproj_o[:, k * 96 : (k + 1) * 96] = value[:, :96] * scale

    zo.stage6(put_taps(gout_o, ((3, 4, 0, 1, 2), (5, 6, 7, 8))))
    zi.stage6(put_taps(gin_o, ((3, 0, 1, 2), (4, 5, 6, 7, 8))))
    zp.stage6(put_project)

    for c in act_halo + hid_halo + cot_halo + bh_halo + cot_copies + refined_copies:
        c.wait_send()
    for p in (o1, o2, i1, i2, pp, zo, zi, zp):
        p.finish()
    gtok_copy.wait()
    refined_copy.wait()


def hand_over(*refs):
    src, dst, via, sem = refs[:5], refs[5:10], refs[10:15], refs[15]
    into = [pltpu.make_async_copy(src[k], via[k], sem.at[k]) for k in range(5)]
    out = [pltpu.make_async_copy(via[k], dst[k], sem.at[5 + k]) for k in range(5)]
    for c in into:
        c.start()
    for k in (0, 2, 3, 4, 1):
        into[k].wait()
        out[k].start()
    for c in out:
        c.wait()


def shards(tokens, wp, bp, wi, bi, wo, bo, cot):
    scale = 1.0 / math.sqrt(COLS * TILE_ROWS * NROW)
    table = scratch_table()
    hbm = pl.BlockSpec(memory_space=pl.ANY)
    vmem = pl.BlockSpec(memory_space=pltpu.VMEM)
    share, width = DIM // NCOL, DIM // NROW

    def body(*refs):
        kernel(list(table), scale, *refs)

    shapes = (
        jax.ShapeDtypeStruct((TILE_ROWS, TILE_COLS, DIM), BF),
        jax.ShapeDtypeStruct((TOK, VIT), BF),
        jax.ShapeDtypeStruct((share, VIT // NROW), F32),
        jax.ShapeDtypeStruct((9, share, width), F32),
        jax.ShapeDtypeStruct((9, share, width), F32),
    )
    results = pl.pallas_call(
        body,
        out_shape=shapes,
        in_specs=[hbm, hbm, vmem, hbm, vmem, hbm, vmem, hbm],
        out_specs=(hbm, hbm, vmem, vmem, vmem),
        scratch_shapes=list(table.values()),
        compiler_params=pltpu.CompilerParams(
            collective_id=0, has_side_effects=True, vmem_limit_bytes=60 * 1024 * 1024
        ),
        name="refine_unit",
    )(tokens, wp, bp, wi.reshape(3, WIDE, DIM), bi, wo.reshape(3, WIDE, DIM), bo, cot)
    refined, gtok, gproj, gin, gout = pl.pallas_call(
        hand_over,
        out_shape=shapes,
        in_specs=[hbm] * 5,
        out_specs=(hbm,) * 5,
        scratch_shapes=[pltpu.VMEM(v.shape, v.dtype) for v in shapes] + [pltpu.SemaphoreType.DMA((10,))],
        name="hand_over",
    )(*results)
    turn = lambda g: g.reshape(3, 3, share, width).transpose(0, 1, 3, 2)
    return refined, gtok, gproj.T, turn(gin), turn(gout)


def solution(mesh):
    in_specs = (
        P(("frame", "row", "col"), None),
        P(),
        P(),
        P(),
        P(),
        P(),
        P(),
        P(("frame", "row"), "col", None),
    )
    out_specs = (
        P(("frame", "row"), "col", None),
        P(("frame", "row", "col"), None),
        P(("frame", "row"), "col"),
        P("frame", None, "row", "col"),
        P("frame", None, "row", "col"),
    )
    return jax.shard_map(shards, mesh=mesh, in_specs=in_specs, out_specs=out_specs, check_vma=False)
```

```python
import math

import jax
import jax.numpy as jnp
from jax import lax
from jax.experimental import pallas as pl
from jax.experimental.pallas import tpu as pltpu
from jax.sharding import PartitionSpec as P

VIT = 1536
DIM = 384
WIDE = 3 * DIM
COLS = 256
TOK = 512
TILE_ROWS = 32
TILE_COLS = 16
NY = 4
NX = 2
NZ = 8
NCOL = 16
NROW = 8
BF = jnp.bfloat16
F32 = jnp.float32
MESH = pl.DeviceIdType.MESH

ROW_PIECES = (
    ("o1", 96, 48, (3, 4, 5)),
    ("o2", 144, 144, (0, 1, 2, 6, 7, 8)),
    ("i1", 48, 96, (3, 4, 5)),
    ("i2", 144, 144, (0, 1, 2, 6, 7, 8)),
    ("p", 96, 96, ()),
)
Z_PIECES = (("zo", 256), ("zi", 256), ("zp", 128))
CORE, XAX, YAX, NROWSEM = 0, 1, 2, 8
SWAP, NZSEM = 7, 8


def scratch_table():
    table = {
        "tok": ((TOK, VIT), BF),
        "tok_t": ((VIT, TOK), BF),
        "wp": ((VIT, DIM), BF),
        "wi": ((3, WIDE, DIM), BF),
        "wo": ((3, WIDE, DIM), BF),
        "act": ((4, COLS, DIM), BF),
        "hid": ((4, COLS, DIM), BF),
        "cot": ((4, COLS, DIM), BF),
        "bh": ((4, COLS, DIM), BF),
        "ea": ((4 * COLS, WIDE), BF),
        "eh": ((4 * COLS, WIDE), BF),
        "ec": ((4 * COLS, WIDE), BF),
        "feat": ((TOK, DIM), BF),
        "bf": ((TOK, DIM), BF),
        "slope": ((TOK, DIM), F32),
        "acc": ((TOK, DIM), F32),
        "acc_t": ((TOK, DIM), F32),
        "bp": ((DIM,), F32),
        "bi": ((DIM,), F32),
        "bo": ((DIM,), F32),
        "act_t": ((DIM, TOK), BF),
        "hid_t": ((DIM, TOK), BF),
        "strip": ((2, COLS, DIM), BF),
        "tile": ((TILE_ROWS, TILE_COLS, DIM), BF),
        "gtok": ((TOK, VIT), BF),
    }
    for name, n0, n1, _ in ROW_PIECES:
        nm = max(n0, n1)
        table |= {
            name + "_part": ((NROW, n0 + n1, DIM), BF),
            name + "_core": ((NROW, nm, DIM), BF),
            name + "_sum": ((NY, NX, nm, DIM), BF),
            name + "_xr": ((NY, nm, DIM), BF),
            name + "_sx": ((NY, nm, DIM), BF),
            name + "_yr": ((6, nm, DIM), BF),
            name + "_fw": ((2, nm, DIM), BF),
        }
    for name, lanes in Z_PIECES:
        table |= {
            name + "_red": ((lanes, DIM), F32),
            name + "_zs": ((NZ, DIM // NZ, lanes), BF),
            name + "_zr": ((NZ - 1, DIM // NZ, lanes), BF),
            name + "_fs": ((2, DIM // NCOL, lanes), F32),
            name + "_fr": ((DIM // NCOL, lanes), F32),
        }
    out = {k: pltpu.VMEM(*v) for k, v in table.items()}
    for group, count in ((ROW_PIECES, NROWSEM), (Z_PIECES, NZSEM)):
        for piece in group:
            out[piece[0] + "_ss"] = pltpu.SemaphoreType.DMA((count,))
            out[piece[0] + "_rs"] = pltpu.SemaphoreType.DMA((count,))
    out["load"] = pltpu.SemaphoreType.DMA((11,))
    out["halo_ss"] = pltpu.SemaphoreType.DMA((8,))
    out["halo_rs"] = pltpu.SemaphoreType.DMA((8,))
    out["swap_ss"] = pltpu.SemaphoreType.DMA((30,))
    out["swap_rs"] = pltpu.SemaphoreType.DMA((30,))
    return out


def dot(a, b):
    return jnp.dot(a, b, preferred_element_type=F32)


def dot_nt(a, b):
    return lax.dot_general(a, b, (((1,), (1,)), ((), ())), preferred_element_type=F32)


def silu(v):
    return v * jax.nn.sigmoid(v)


def silu_slope(v):
    s = jax.nn.sigmoid(v)
    return s * (1.0 + v * (1.0 - s))


class Where:
    def __init__(self):
        self.r = lax.axis_index("row")
        self.c = lax.axis_index("col")
        self.y = self.r // 2
        self.x = self.r % 2
        self.z = self.c // 2
        self.core = self.c % 2
        here = self.r * NCOL + self.c
        above = (here + NROW * NCOL - 1) % (NROW * NCOL)
        below = (here + 1) % (NROW * NCOL)
        self.up = {"row": above // NCOL, "col": above % NCOL}
        self.down = {"row": below // NCOL, "col": below % NCOL}
        self.first = here == 0
        self.last = here == NROW * NCOL - 1
        self.pair = {"col": self.z * 2 + 1 - self.core}
        self.across = {"row": self.y * 2 + 1 - self.x}

    def at_y(self, k):
        return {"row": ((self.y + k) % NY) * 2 + self.x}

    def at_z(self, k):
        return {"col": ((self.z + k) % NZ) * 2 + self.core}

    def at_col(self, k):
        return {"col": (self.c + k) % NCOL}


def remote(src, dst, ss, rs, device):
    return pltpu.make_async_remote_copy(
        src_ref=src, dst_ref=dst, send_sem=ss, recv_sem=rs, device_id=device, device_id_type=MESH
    )


def per_core(w, step):
    for k in (0, 1):
        pl.when(w.core == k)(lambda k=k: step(k))


class RowPiece:
    def __init__(self, w, m, name, n0, n1, red, at):
        self.w = w
        self.n = (n0, n1)
        self.off = (0, n0)
        self.out = (red, at)
        for field in ("part", "core", "sum", "xr", "sx", "yr", "fw", "ss", "rs"):
            setattr(self, field, m[name + "_" + field])

    def copy(self, src, dst, k, device):
        return remote(src, dst, self.ss.at[k], self.rs.at[k], device)

    def core_out(self, k):
        o, m = self.off[1 - k], self.n[1 - k]
        return self.copy(self.part.at[:, o : o + m], self.core.at[:, :m], CORE, self.w.pair)

    def core_in(self, k):
        n = self.n[k]
        return self.copy(self.core.at[:, :n], self.core.at[:, :n], CORE, self.w.pair)

    def stage0(self):
        per_core(self.w, lambda k: self.core_out(k).start())

    def x_copy(self, k):
        n = self.n[k]
        if k == 0:
            src, dst = self.sum.at[:, 1 - self.w.x, :n], self.xr.at[:, :n]
        else:
            src, dst = self.sx.at[1 - self.w.x, :n], self.xr.at[0, :n]
        return self.copy(src, dst, XAX, self.w.across)

    def halves(self, k):
        n = self.n[k]
        if k == 1:
            return (pl.ds(0, n), pl.ds(0, n))
        low = (n // 32) * 16
        return (pl.ds(0, low), pl.ds(low, n - low))

    def block(self, k, t, h):
        if k == 1:
            return self.sum.at[t, h, pl.ds(0, self.n[1])]
        return self.sx.at[t, self.halves(0)[h]]

    def slot(self, k, s, h):
        return self.yr.at[s, pl.ds(0, self.halves(k)[h].size)]

    def forward(self, k, h):
        return self.fw.at[h, pl.ds(0, self.halves(k)[h].size)]

    def y_copy(self, k, j):
        w = self.w
        far, before, after = (w.y + 2) % NY, (w.y + 3) % NY, (w.y + 1) % NY
        h = j % 2
        step = (1, 3, 3, 1, 1, 3)[j]
        if j < 4:
            src = self.block(k, (far, far, before, after)[j], h)
        else:
            src = self.forward(k, h)
        return self.copy(src, self.slot(k, j, h), YAX + j, w.at_y(step))

    def y_first(self, k):
        for j in range(4):
            self.y_copy(k, j).start()

    def y_second(self, k):
        for h, t in ((0, (self.w.y + 1) % NY), (1, (self.w.y + 3) % NY)):
            self.y_copy(k, h).wait_recv()
            self.forward(k, h)[...] = self.block(k, t, h)[...] + self.slot(k, h, h)[...]
            self.y_copy(k, 4 + h).start()

    def y_end(self, k, h):
        self.y_copy(k, 2 + h).wait_recv()
        self.y_copy(k, 4 + h).wait_recv()
        return (
            self.block(k, self.w.y, h)[...].astype(F32)
            + self.slot(k, 4 + h, h)[...].astype(F32)
            + self.slot(k, 2 + h, h)[...].astype(F32)
        )

    def stage1(self):
        def step(k):
            n, o = self.n[k], self.off[k]
            self.core_in(k).wait_recv()
            for j in range(NROW):
                self.sum[j // NX, j % NX, :n] = self.part[j, o : o + n] + self.core[j, :n]
            if k == 0:
                self.x_copy(0).start()
            else:
                self.y_first(1)

        per_core(self.w, step)

    def stage2(self):
        def step(k):
            if k == 0:
                n = self.n[0]
                self.x_copy(0).wait_recv()
                for t in range(NY):
                    self.sx[t, :n] = self.sum[t, self.w.x, :n] + self.xr[t, :n]
                self.y_first(0)
            else:
                self.y_second(1)

        per_core(self.w, step)

    def stage3(self):
        def step(k):
            if k == 0:
                self.y_second(0)
            else:
                for h in (0, 1):
                    self.sx[h, : self.n[1]] = self.y_end(1, h).astype(BF)
                self.x_copy(1).start()

        per_core(self.w, step)

    def stage4(self):
        def step(k):
            red, at = self.out[0], self.out[1][k]
            n = self.n[k]
            if k == 0:
                for h in (0, 1):
                    rows = self.halves(0)[h]
                    red[at + rows.start : at + rows.start + rows.size] = self.y_end(0, h)
            else:
                self.x_copy(1).wait_recv()
                red[at : at + n] = self.sx[self.w.x, :n].astype(F32) + self.xr[0, :n].astype(F32)

        per_core(self.w, step)

    def finish(self):
        def step(k):
            self.core_out(k).wait_send()
            self.x_copy(k).wait_send()
            for j in range(6):
                self.y_copy(k, j).wait_send()

        per_core(self.w, step)


class ZPiece:
    def __init__(self, w, m, name, lanes, rows):
        self.w = w
        self.lanes = lanes
        self.rows = rows
        for field in ("red", "zs", "zr", "fs", "fr", "ss", "rs"):
            setattr(self, field, m[name + "_" + field])

    def copy(self, d):
        w = self.w
        if d == 0:
            src, dst, k, device = self.fs.at[1 - w.core], self.fr, SWAP, w.pair
        else:
            src, dst, k, device = self.zs.at[(w.z + d) % NZ], self.zr.at[d - 1], d - 1, w.at_z(d)
        return remote(src, dst, self.ss.at[k], self.rs.at[k], device)

    def clear(self):
        low = min(self.rows)
        self.red[low:] = jnp.zeros((self.lanes - low, DIM), F32)

    def stage4(self):
        self.zs[...] = self.red[...].T.astype(BF).reshape(NZ, DIM // NZ, self.lanes)
        for d in (4, 3, 5, 2, 6, 1, 7):
            self.copy(d).start()

    def stage5(self):
        total = self.zs[self.w.z].astype(F32)
        for d in range(1, NZ):
            self.copy(d).wait_recv()
            total = total + self.zr[d - 1].astype(F32)
        self.fs[...] = total.reshape(2, DIM // NCOL, self.lanes)
        self.copy(0).start()

    def stage6(self, put):
        self.copy(0).wait_recv()

        def step(k):
            put(k, self.fs[k])
            put(1 - k, self.fr[...])

        per_core(self.w, step)

    def finish(self):
        for d in range(NZ):
            self.copy(d).wait_send()


def kernel(names, scale, *refs):
    tok_h, wp_h, bp_h, wi_h, bi_h, wo_h, bo_h, cot_h = refs[:8]
    refined_o, gtok_o, gproj_o, gin_o, gout_o = refs[8:13]
    m = dict(zip(names, refs[13:]))
    w = Where()
    share, width = DIM // NCOL, DIM // NROW
    zo = ZPiece(w, m, "zo", 256, (240, 192))
    zi = ZPiece(w, m, "zi", 256, (192, 240))
    zp = ZPiece(w, m, "zp", 128, (96, 96))
    places = {"o1": (zo, (0, 0)), "o2": (zo, (96, 48)), "i1": (zi, (0, 0)), "i2": (zi, (48, 96)), "p": (zp, (0, 0))}
    rows, taps = {}, {}
    for name, n0, n1, taps[name] in ROW_PIECES:
        target, at = places[name]
        rows[name] = RowPiece(w, m, name, n0, n1, target.red, at)
    o1, o2, i1, i2, pp = rows.values()

    barrier = pltpu.get_barrier_semaphore()
    friends = [w.at_col(k) for k in range(1, NCOL)]
    friends += [w.across, w.at_y(1), w.at_y(3), w.up, w.down]
    for device in friends:
        pl.semaphore_signal(barrier, inc=1, device_id=device, device_id_type=MESH)

    load = m["load"]
    sources = {"tok": tok_h, "wp": wp_h, "bp": bp_h, "wi": wi_h, "bi": bi_h, "wo": wo_h, "bo": bo_h}
    loads = {
        name: pltpu.make_async_copy(src, m[name], load.at[k])
        for k, (name, src) in enumerate(sources.items())
    }
    for name in ("tok", "wp", "bp", "bi", "bo"):
        loads[name].start()
    here = pl.ds(pl.multiple_of(w.c * TILE_COLS, TILE_COLS), TILE_COLS)
    mine = pl.ds(w.c * 2, 2)
    cot = m["cot"]

    def halo(center, k):
        up = remote(center.at[1], center.at[3], m["halo_ss"].at[k], m["halo_rs"].at[k], w.up)
        down = remote(center.at[2], center.at[0], m["halo_ss"].at[k + 1], m["halo_rs"].at[k + 1], w.down)
        up.start()
        down.start()
        return [down, up]

    keep_low = jnp.where(w.first, 0.0, 1.0).astype(F32)
    keep_high = jnp.where(w.last, 0.0, 1.0).astype(F32)

    def expand(center, wide, row, flip):
        v = center[row].astype(F32)
        if row == 0:
            v = v * keep_low
        if row == 3:
            v = v * keep_high
        at = lax.broadcasted_iota(jnp.int32, (COLS, DIM), 0)
        before = jnp.where(at == 0, 0.0, pltpu.roll(v, 1, 0))
        after = jnp.where(at == COLS - 1, 0.0, pltpu.roll(v, COLS - 1, 0))
        first, last = (after, before) if flip else (before, after)
        rows = pl.ds(row * COLS, COLS)
        wide[rows, 0:DIM] = first.astype(BF)
        wide[rows, DIM : 2 * DIM] = v.astype(BF)
        wide[rows, 2 * DIM : WIDE] = last.astype(BF)

    def expand_rim(center, wide, copies, flip):
        copies[0].wait_recv()
        expand(center, wide, 0, flip)
        copies[1].wait_recv()
        expand(center, wide, 3, flip)

    acc, acc_t = m["acc"], m["acc_t"]
    first, second = slice(0, COLS), slice(COLS, TOK)

    def row(wide, k):
        return wide[k * COLS : (k + 1) * COLS]

    def conv_inner(wide, kern):
        acc[...] = dot(wide[COLS : 3 * COLS], kern[1])
        acc[first] += dot(row(wide, 2), kern[2])
        acc[second] += dot(row(wide, 1), kern[0])

    def conv_rim(wide, kern):
        acc[first] += dot(row(wide, 0), kern[0])
        acc[second] += dot(row(wide, 3), kern[2])

    def taps_t(wide, k0, k1, kern, a):
        total = None
        for b in range(3):
            lanes = slice(b * DIM, (b + 1) * DIM)
            term = dot_nt(wide[k0 * COLS : k1 * COLS, lanes], kern[a, lanes])
            total = term if total is None else total + term
        return total

    def conv_t_inner(wide, kern):
        acc_t[...] = taps_t(wide, 1, 3, kern, 1)
        acc_t[first] += taps_t(wide, 2, 3, kern, 0)
        acc_t[second] += taps_t(wide, 1, 2, kern, 2)

    def conv_t_rim(wide, kern):
        acc_t[first] += taps_t(wide, 0, 1, kern, 2)
        acc_t[second] += taps_t(wide, 3, 4, kern, 0)

    def weight_grad(left_t, wide, name):
        for a in sorted({t // 3 for t in taps[name]}):
            g = dot(left_t[...], wide[(2 - a) * COLS : (2 - a) * COLS + TOK])
            for b in range(3):
                at = taps[name].index(3 * a + b) * width
                rows[name].part[:, at : at + width] = (
                    g[:, b * DIM : (b + 1) * DIM].astype(BF).reshape(NROW, width, DIM)
                )

    pl.semaphore_wait(barrier, len(friends))
    turn = [8, 7, 9, 6, 10, 5, 11, 4, 12, 3, 13, 2, 14, 1, 15]
    cot_copies = []
    for k in turn:
        there = (w.c + k) % NCOL
        cot_copies.append(
            remote(
                cot_h.at[pl.ds(there * 2, 2)],
                cot.at[pl.ds(1, 2), here],
                m["swap_ss"].at[k - 1],
                m["swap_rs"].at[k - 1],
                w.at_col(k),
            )
        )
        cot_copies[-1].start()
    own_cot = pltpu.make_async_copy(cot_h.at[mine], cot.at[pl.ds(1, 2), here], load.at[7])
    own_cot.start()

    act, hid, bh = m["act"], m["hid"], m["bh"]
    for name in ("tok", "wp", "bp"):
        loads[name].wait()
    loads["wi"].start()
    feature = (dot(m["tok"][...], m["wp"][...]) + m["bp"][...][None, :]).astype(BF)
    m["feat"][...] = feature
    act[1:3] = silu(feature.astype(F32)).astype(BF).reshape(2, COLS, DIM)
    act_halo = halo(act, 0)
    loads["wo"].start()
    for z in (zo, zi, zp):
        z.clear()
    expand(act, m["ea"], 1, False)
    expand(act, m["ea"], 2, False)

    loads["wi"].wait()
    conv_inner(m["ea"], m["wi"])
    m["act_t"][...] = act[1:3].reshape(TOK, DIM).T
    m["tok_t"][...] = m["tok"][...].T

    own_cot.wait()
    for c in cot_copies:
        c.wait_recv()
    cot_halo = halo(cot, 4)
    expand(cot, m["ec"], 1, True)
    expand(cot, m["ec"], 2, True)
    loads["wo"].wait()
    conv_t_inner(m["ec"], m["wo"])
    expand_rim(act, m["ea"], act_halo, False)
    conv_rim(m["ea"], m["wi"])
    loads["bi"].wait()
    pre = acc[...] + m["bi"][...][None, :]
    hid[1:3] = silu(pre).astype(BF).reshape(2, COLS, DIM)
    m["slope"][...] = silu_slope(pre)
    m["hid_t"][...] = hid[1:3].reshape(TOK, DIM).T
    weight_grad(m["hid_t"], m["ec"], "o1")
    o1.stage0()
    expand_rim(cot, m["ec"], cot_halo, True)

    conv_t_rim(m["ec"], m["wo"])
    bh[1:3] = (acc_t[...] * m["slope"][...]).astype(BF).reshape(2, COLS, DIM)
    bh_halo = halo(bh, 6)
    weight_grad(m["hid_t"], m["ec"], "o2")
    o2.stage0()
    o1.stage1()
    expand(bh, m["ea"], 1, True)
    expand(bh, m["ea"], 2, True)
    weight_grad(m["act_t"], m["ea"], "i1")
    i1.stage0()
    conv_t_inner(m["ea"], m["wi"])
    o2.stage1()
    expand_rim(bh, m["ea"], bh_halo, True)
    hid_halo = halo(hid, 2)

    weight_grad(m["act_t"], m["ea"], "i2")
    i2.stage0()
    i1.stage1()
    conv_t_rim(m["ea"], m["wi"])
    back = acc_t[...] * silu_slope(m["feat"][...].astype(F32))
    m["bf"][...] = (cot[1:3].reshape(TOK, DIM).astype(F32) + back).astype(BF)
    o1.stage2()
    pp.part[...] = dot(m["tok_t"][...], m["bf"][...]).astype(BF).reshape(NROW, VIT // NROW, DIM)
    pp.stage0()
    i2.stage1()
    o2.stage2()
    pp.stage1()
    o1.stage3()

    expand(hid, m["eh"], 1, False)
    expand(hid, m["eh"], 2, False)
    conv_inner(m["eh"], m["wo"])
    o1.stage4()
    expand_rim(hid, m["eh"], hid_halo, False)
    conv_rim(m["eh"], m["wo"])
    loads["bo"].wait()
    refined = m["feat"][...].astype(F32) + acc[...] + m["bo"][...][None, :]
    m["strip"][...] = refined.astype(BF).reshape(2, COLS, DIM)
    refined_copies = []
    for k in turn:
        there = (w.c + k) % NCOL
        refined_copies.append(
            remote(
                m["strip"].at[:, pl.ds(pl.multiple_of(there * TILE_COLS, TILE_COLS), TILE_COLS)],
                m["tile"].at[mine],
                m["swap_ss"].at[14 + k],
                m["swap_rs"].at[14 + k],
                w.at_col(k),
            )
        )
        refined_copies[-1].start()
    own_refined = pltpu.make_async_copy(m["strip"].at[:, here], m["tile"].at[mine], load.at[8])
    own_refined.start()
    i1.stage2()
    o2.stage3()
    m["gtok"][...] = dot_nt(m["bf"][...], m["wp"][...]).astype(BF)
    gtok_copy = pltpu.make_async_copy(m["gtok"], gtok_o, load.at[9])
    gtok_copy.start()
    i1.stage3()
    i2.stage2()
    o2.stage4()
    zo.stage4()
    i1.stage4()
    pp.stage2()
    i2.stage3()
    pp.stage3()
    i2.stage4()
    zi.stage4()
    pp.stage4()
    zp.stage4()
    zo.stage5()
    own_refined.wait()
    for c in refined_copies:
        c.wait_recv()
    refined_copy = pltpu.make_async_copy(m["tile"], refined_o, load.at[10])
    refined_copy.start()
    zi.stage5()
    zp.stage5()

    def put_taps(out, order):
        def put(k, value):
            for j, t in enumerate(order[k]):
                out[t] = value[:, j * width : (j + 1) * width] * scale

        return put

    def put_project(k, value):
        gproj_o[:, k * 96 : (k + 1) * 96] = value[:, :96] * scale

    zo.stage6(put_taps(gout_o, ((3, 4, 0, 1, 2), (5, 6, 7, 8))))
    zi.stage6(put_taps(gin_o, ((3, 0, 1, 2), (4, 5, 6, 7, 8))))
    zp.stage6(put_project)

    for c in act_halo + hid_halo + cot_halo + bh_halo + cot_copies + refined_copies:
        c.wait_send()
    for p in (o1, o2, i1, i2, pp, zo, zi, zp):
        p.finish()
    gtok_copy.wait()
    refined_copy.wait()


def hand_over(*refs):
    src, dst, via, sem = refs[:5], refs[5:10], refs[10:15], refs[15]
    part = TOK // 4
    views = [[ref.at[pl.ds(j * part, part)] for j in range(4)] for ref in (src[1], via[1], dst[1])]
    for k, group in enumerate((src, via, dst)):
        views[k] += [group[j] for j in (0, 2, 3, 4)]
    into = [pltpu.make_async_copy(views[0][k], views[1][k], sem.at[k]) for k in range(8)]
    out = [pltpu.make_async_copy(views[1][k], views[2][k], sem.at[8 + k]) for k in range(8)]
    for c in into:
        c.start()
    for k in range(8):
        into[k].wait()
        out[k].start()
    for c in out:
        c.wait()


def shards(tokens, wp, bp, wi, bi, wo, bo, cot):
    scale = 1.0 / math.sqrt(COLS * TILE_ROWS * NROW)
    table = scratch_table()
    hbm = pl.BlockSpec(memory_space=pl.ANY)
    vmem = pl.BlockSpec(memory_space=pltpu.VMEM)
    share, width = DIM // NCOL, DIM // NROW

    def body(*refs):
        kernel(list(table), scale, *refs)

    shapes = (
        jax.ShapeDtypeStruct((TILE_ROWS, TILE_COLS, DIM), BF),
        jax.ShapeDtypeStruct((TOK, VIT), BF),
        jax.ShapeDtypeStruct((share, VIT // NROW), F32),
        jax.ShapeDtypeStruct((9, share, width), F32),
        jax.ShapeDtypeStruct((9, share, width), F32),
    )
    results = pl.pallas_call(
        body,
        out_shape=shapes,
        in_specs=[hbm] * 8,
        out_specs=(hbm, hbm, vmem, vmem, vmem),
        scratch_shapes=list(table.values()),
        compiler_params=pltpu.CompilerParams(
            collective_id=0, has_side_effects=True, vmem_limit_bytes=60 * 1024 * 1024
        ),
        name="refine_unit",
    )(tokens, wp, bp, wi.reshape(3, WIDE, DIM), bi, wo.reshape(3, WIDE, DIM), bo, cot)
    refined, gtok, gproj, gin, gout = pl.pallas_call(
        hand_over,
        out_shape=shapes,
        in_specs=[hbm] * 5,
        out_specs=(hbm,) * 5,
        scratch_shapes=[pltpu.VMEM(v.shape, v.dtype) for v in shapes] + [pltpu.SemaphoreType.DMA((16,))],
        name="hand_over",
    )(*results)
    turn = lambda g: g.reshape(3, 3, share, width).transpose(0, 1, 3, 2)
    return refined, gtok, gproj.T, turn(gin), turn(gout)


def solution(mesh):
    in_specs = (
        P(("frame", "row", "col"), None),
        P(),
        P(),
        P(),
        P(),
        P(),
        P(),
        P(("frame", "row"), "col", None),
    )
    out_specs = (
        P(("frame", "row"), "col", None),
        P(("frame", "row", "col"), None),
        P(("frame", "row"), "col"),
        P("frame", None, "row", "col"),
        P("frame", None, "row", "col"),
    )
    return jax.shard_map(shards, mesh=mesh, in_specs=in_specs, out_specs=out_specs, check_vma=False)
```

```python
import math

import jax
import jax.numpy as jnp
from jax import lax
from jax.experimental import pallas as pl
from jax.experimental.pallas import tpu as pltpu
from jax.sharding import PartitionSpec as P

VIT = 1536
DIM = 384
WIDE = 3 * DIM
COLS = 256
TOK = 512
TILE_ROWS = 32
TILE_COLS = 16
NY = 4
NX = 2
NZ = 8
NCOL = 16
NROW = 8
BF = jnp.bfloat16
F32 = jnp.float32
MESH = pl.DeviceIdType.MESH

ROW_PIECES = (
    ("o1", 96, 48, (3, 4, 5)),
    ("o2", 144, 144, (0, 1, 2, 6, 7, 8)),
    ("i1", 48, 96, (3, 4, 5)),
    ("i2", 144, 144, (0, 1, 2, 6, 7, 8)),
    ("p", 96, 96, ()),
)
Z_PIECES = (("zo", 256), ("zi", 256), ("zp", 128))
CORE, XAX, YAX, NROWSEM = 0, 1, 2, 8
SWAP, NZSEM = 7, 8


def scratch_table():
    table = {
        "tok": ((TOK, VIT), BF),
        "tok_t": ((VIT, TOK), BF),
        "wp": ((VIT, DIM), BF),
        "wi": ((3, WIDE, DIM), BF),
        "wo": ((3, WIDE, DIM), BF),
        "act": ((4, COLS, DIM), BF),
        "hid": ((4, COLS, DIM), BF),
        "cot": ((4, COLS, DIM), BF),
        "bh": ((4, COLS, DIM), BF),
        "ea": ((4 * COLS, WIDE), BF),
        "eh": ((4 * COLS, WIDE), BF),
        "ec": ((4 * COLS, WIDE), BF),
        "feat": ((TOK, DIM), BF),
        "bf": ((TOK, DIM), BF),
        "slope": ((TOK, DIM), F32),
        "acc": ((TOK, DIM), F32),
        "acc_t": ((TOK, DIM), F32),
        "bp": ((DIM,), F32),
        "bi": ((DIM,), F32),
        "bo": ((DIM,), F32),
        "act_t": ((DIM, TOK), BF),
        "hid_t": ((DIM, TOK), BF),
        "strip": ((2, COLS, DIM), BF),
        "tile": ((TILE_ROWS, TILE_COLS, DIM), BF),
        "gtok": ((TOK, VIT), BF),
    }
    for name, n0, n1, _ in ROW_PIECES:
        nm = max(n0, n1)
        table |= {
            name + "_part": ((NROW, n0 + n1, DIM), BF),
            name + "_core": ((NROW, nm, DIM), BF),
            name + "_sum": ((NY, NX, nm, DIM), BF),
            name + "_xr": ((NY, nm, DIM), BF),
            name + "_sx": ((NY, nm, DIM), BF),
            name + "_yr": ((6, nm, DIM), BF),
            name + "_fw": ((2, nm, DIM), BF),
        }
    for name, lanes in Z_PIECES:
        table |= {
            name + "_red": ((lanes, DIM), F32),
            name + "_zs": ((NZ, DIM // NZ, lanes), BF),
            name + "_zr": ((NZ - 1, DIM // NZ, lanes), BF),
            name + "_fs": ((2, DIM // NCOL, lanes), F32),
            name + "_fr": ((DIM // NCOL, lanes), F32),
        }
    out = {k: pltpu.VMEM(*v) for k, v in table.items()}
    for group, count in ((ROW_PIECES, NROWSEM), (Z_PIECES, NZSEM)):
        for piece in group:
            out[piece[0] + "_ss"] = pltpu.SemaphoreType.DMA((count,))
            out[piece[0] + "_rs"] = pltpu.SemaphoreType.DMA((count,))
    out["load"] = pltpu.SemaphoreType.DMA((11,))
    out["halo_ss"] = pltpu.SemaphoreType.DMA((8,))
    out["halo_rs"] = pltpu.SemaphoreType.DMA((8,))
    out["swap_ss"] = pltpu.SemaphoreType.DMA((30,))
    out["swap_rs"] = pltpu.SemaphoreType.DMA((30,))
    return out


def dot(a, b):
    return jnp.dot(a, b, preferred_element_type=F32)


def dot_nt(a, b):
    return lax.dot_general(a, b, (((1,), (1,)), ((), ())), preferred_element_type=F32)


def silu(v):
    return v * jax.nn.sigmoid(v)


def silu_slope(v):
    s = jax.nn.sigmoid(v)
    return s * (1.0 + v * (1.0 - s))


class Where:
    def __init__(self):
        self.r = lax.axis_index("row")
        self.c = lax.axis_index("col")
        self.y = self.r // 2
        self.x = self.r % 2
        self.z = self.c // 2
        self.core = self.c % 2
        here = self.r * NCOL + self.c
        above = (here + NROW * NCOL - 1) % (NROW * NCOL)
        below = (here + 1) % (NROW * NCOL)
        self.up = {"row": above // NCOL, "col": above % NCOL}
        self.down = {"row": below // NCOL, "col": below % NCOL}
        self.first = here == 0
        self.last = here == NROW * NCOL - 1
        self.pair = {"col": self.z * 2 + 1 - self.core}
        self.across = {"row": self.y * 2 + 1 - self.x}

    def at_y(self, k):
        return {"row": ((self.y + k) % NY) * 2 + self.x}

    def at_z(self, k):
        return {"col": ((self.z + k) % NZ) * 2 + self.core}

    def at_col(self, k):
        return {"col": (self.c + k) % NCOL}


def remote(src, dst, ss, rs, device):
    return pltpu.make_async_remote_copy(
        src_ref=src, dst_ref=dst, send_sem=ss, recv_sem=rs, device_id=device, device_id_type=MESH
    )


def per_core(w, step):
    for k in (0, 1):
        pl.when(w.core == k)(lambda k=k: step(k))


class RowPiece:
    def __init__(self, w, m, name, n0, n1, red, at):
        self.w = w
        self.n = (n0, n1)
        self.off = (0, n0)
        self.out = (red, at)
        for field in ("part", "core", "sum", "xr", "sx", "yr", "fw", "ss", "rs"):
            setattr(self, field, m[name + "_" + field])

    def copy(self, src, dst, k, device):
        return remote(src, dst, self.ss.at[k], self.rs.at[k], device)

    def core_out(self, k):
        o, m = self.off[1 - k], self.n[1 - k]
        return self.copy(self.part.at[:, o : o + m], self.core.at[:, :m], CORE, self.w.pair)

    def core_in(self, k):
        n = self.n[k]
        return self.copy(self.core.at[:, :n], self.core.at[:, :n], CORE, self.w.pair)

    def stage0(self):
        per_core(self.w, lambda k: self.core_out(k).start())

    def x_copy(self, k):
        n = self.n[k]
        if k == 0:
            src, dst = self.sum.at[:, 1 - self.w.x, :n], self.xr.at[:, :n]
        else:
            src, dst = self.sx.at[1 - self.w.x, :n], self.xr.at[0, :n]
        return self.copy(src, dst, XAX, self.w.across)

    def halves(self, k):
        n = self.n[k]
        if k == 1:
            return (pl.ds(0, n), pl.ds(0, n))
        low = (n // 32) * 16
        return (pl.ds(0, low), pl.ds(low, n - low))

    def block(self, k, t, h):
        if k == 1:
            return self.sum.at[t, h, pl.ds(0, self.n[1])]
        return self.sx.at[t, self.halves(0)[h]]

    def slot(self, k, s, h):
        return self.yr.at[s, pl.ds(0, self.halves(k)[h].size)]

    def forward(self, k, h):
        return self.fw.at[h, pl.ds(0, self.halves(k)[h].size)]

    def y_copy(self, k, j):
        w = self.w
        far, before, after = (w.y + 2) % NY, (w.y + 3) % NY, (w.y + 1) % NY
        h = j % 2
        step = (1, 3, 3, 1, 1, 3)[j]
        if j < 4:
            src = self.block(k, (far, far, before, after)[j], h)
        else:
            src = self.forward(k, h)
        return self.copy(src, self.slot(k, j, h), YAX + j, w.at_y(step))

    def y_first(self, k):
        for j in range(4):
            self.y_copy(k, j).start()

    def y_second(self, k):
        for h, t in ((0, (self.w.y + 1) % NY), (1, (self.w.y + 3) % NY)):
            self.y_copy(k, h).wait_recv()
            self.forward(k, h)[...] = self.block(k, t, h)[...] + self.slot(k, h, h)[...]
            self.y_copy(k, 4 + h).start()

    def y_end(self, k, h):
        self.y_copy(k, 2 + h).wait_recv()
        self.y_copy(k, 4 + h).wait_recv()
        return (
            self.block(k, self.w.y, h)[...].astype(F32)
            + self.slot(k, 4 + h, h)[...].astype(F32)
            + self.slot(k, 2 + h, h)[...].astype(F32)
        )

    def stage1(self):
        def step(k):
            n, o = self.n[k], self.off[k]
            self.core_in(k).wait_recv()
            for j in range(NROW):
                self.sum[j // NX, j % NX, :n] = self.part[j, o : o + n] + self.core[j, :n]
            if k == 0:
                self.x_copy(0).start()
            else:
                self.y_first(1)

        per_core(self.w, step)

    def stage2(self):
        def step(k):
            if k == 0:
                n = self.n[0]
                self.x_copy(0).wait_recv()
                for t in range(NY):
                    self.sx[t, :n] = self.sum[t, self.w.x, :n] + self.xr[t, :n]
                self.y_first(0)
            else:
                self.y_second(1)

        per_core(self.w, step)

    def stage3(self):
        def step(k):
            if k == 0:
                self.y_second(0)
            else:
                for h in (0, 1):
                    self.sx[h, : self.n[1]] = self.y_end(1, h).astype(BF)
                self.x_copy(1).start()

        per_core(self.w, step)

    def stage4(self):
        def step(k):
            red, at = self.out[0], self.out[1][k]
            n = self.n[k]
            if k == 0:
                for h in (0, 1):
                    rows = self.halves(0)[h]
                    red[at + rows.start : at + rows.start + rows.size] = self.y_end(0, h)
            else:
                self.x_copy(1).wait_recv()
                red[at : at + n] = self.sx[self.w.x, :n].astype(F32) + self.xr[0, :n].astype(F32)

        per_core(self.w, step)

    def finish(self):
        def step(k):
            self.core_out(k).wait_send()
            self.x_copy(k).wait_send()
            for j in range(6):
                self.y_copy(k, j).wait_send()

        per_core(self.w, step)


class ZPiece:
    def __init__(self, w, m, name, lanes, rows):
        self.w = w
        self.lanes = lanes
        self.rows = rows
        for field in ("red", "zs", "zr", "fs", "fr", "ss", "rs"):
            setattr(self, field, m[name + "_" + field])

    def copy(self, d):
        w = self.w
        if d == 0:
            src, dst, k, device = self.fs.at[1 - w.core], self.fr, SWAP, w.pair
        else:
            src, dst, k, device = self.zs.at[(w.z + d) % NZ], self.zr.at[d - 1], d - 1, w.at_z(d)
        return remote(src, dst, self.ss.at[k], self.rs.at[k], device)

    def clear(self):
        low = min(self.rows)
        self.red[low:] = jnp.zeros((self.lanes - low, DIM), F32)

    def stage4(self):
        self.zs[...] = self.red[...].T.astype(BF).reshape(NZ, DIM // NZ, self.lanes)
        for d in (4, 3, 5, 2, 6, 1, 7):
            self.copy(d).start()

    def stage5(self):
        total = self.zs[self.w.z].astype(F32)
        for d in range(1, NZ):
            self.copy(d).wait_recv()
            total = total + self.zr[d - 1].astype(F32)
        self.fs[...] = total.reshape(2, DIM // NCOL, self.lanes)
        self.copy(0).start()

    def stage6(self, put):
        self.copy(0).wait_recv()

        def step(k):
            put(k, self.fs[k])
            put(1 - k, self.fr[...])

        per_core(self.w, step)

    def finish(self):
        for d in range(NZ):
            self.copy(d).wait_send()


def kernel(names, scale, *refs):
    tok_h, wp_h, bp_h, wi_h, bi_h, wo_h, bo_h, cot_h = refs[:8]
    refined_o, gtok_o, gproj_o, gin_o, gout_o = refs[8:13]
    m = dict(zip(names, refs[13:]))
    w = Where()
    share, width = DIM // NCOL, DIM // NROW
    zo = ZPiece(w, m, "zo", 256, (240, 192))
    zi = ZPiece(w, m, "zi", 256, (192, 240))
    zp = ZPiece(w, m, "zp", 128, (96, 96))
    places = {"o1": (zo, (0, 0)), "o2": (zo, (96, 48)), "i1": (zi, (0, 0)), "i2": (zi, (48, 96)), "p": (zp, (0, 0))}
    rows, taps = {}, {}
    for name, n0, n1, taps[name] in ROW_PIECES:
        target, at = places[name]
        rows[name] = RowPiece(w, m, name, n0, n1, target.red, at)
    o1, o2, i1, i2, pp = rows.values()

    barrier = pltpu.get_barrier_semaphore()
    friends = [w.at_col(k) for k in range(1, NCOL)]
    friends += [w.across, w.at_y(1), w.at_y(3), w.up, w.down]
    for device in friends:
        pl.semaphore_signal(barrier, inc=1, device_id=device, device_id_type=MESH)

    load = m["load"]
    sources = {"tok": tok_h, "wp": wp_h, "bp": bp_h, "wi": wi_h, "bi": bi_h, "wo": wo_h, "bo": bo_h}
    loads = {
        name: pltpu.make_async_copy(src, m[name], load.at[k])
        for k, (name, src) in enumerate(sources.items())
    }
    for name in ("tok", "wp", "bp", "bi", "bo"):
        loads[name].start()
    here = pl.ds(pl.multiple_of(w.c * TILE_COLS, TILE_COLS), TILE_COLS)
    mine = pl.ds(w.c * 2, 2)
    cot = m["cot"]

    def halo(center, k):
        up = remote(center.at[1], center.at[3], m["halo_ss"].at[k], m["halo_rs"].at[k], w.up)
        down = remote(center.at[2], center.at[0], m["halo_ss"].at[k + 1], m["halo_rs"].at[k + 1], w.down)
        up.start()
        down.start()
        return [down, up]

    keep_low = jnp.where(w.first, 0.0, 1.0).astype(F32)
    keep_high = jnp.where(w.last, 0.0, 1.0).astype(F32)

    def expand(center, wide, row, flip):
        v = center[row].astype(F32)
        if row == 0:
            v = v * keep_low
        if row == 3:
            v = v * keep_high
        at = lax.broadcasted_iota(jnp.int32, (COLS, DIM), 0)
        before = jnp.where(at == 0, 0.0, pltpu.roll(v, 1, 0))
        after = jnp.where(at == COLS - 1, 0.0, pltpu.roll(v, COLS - 1, 0))
        first, last = (after, before) if flip else (before, after)
        rows = pl.ds(row * COLS, COLS)
        wide[rows, 0:DIM] = first.astype(BF)
        wide[rows, DIM : 2 * DIM] = v.astype(BF)
        wide[rows, 2 * DIM : WIDE] = last.astype(BF)

    def expand_rim(center, wide, copies, flip):
        copies[0].wait_recv()
        expand(center, wide, 0, flip)
        copies[1].wait_recv()
        expand(center, wide, 3, flip)

    acc, acc_t = m["acc"], m["acc_t"]
    first, second = slice(0, COLS), slice(COLS, TOK)

    def row(wide, k):
        return wide[k * COLS : (k + 1) * COLS]

    def conv_inner(wide, kern):
        acc[...] = dot(wide[COLS : 3 * COLS], kern[1])
        acc[first] += dot(row(wide, 2), kern[2])
        acc[second] += dot(row(wide, 1), kern[0])

    def conv_rim(wide, kern):
        acc[first] += dot(row(wide, 0), kern[0])
        acc[second] += dot(row(wide, 3), kern[2])

    def taps_t(wide, k0, k1, kern, a):
        total = None
        for b in range(3):
            lanes = slice(b * DIM, (b + 1) * DIM)
            term = dot_nt(wide[k0 * COLS : k1 * COLS, lanes], kern[a, lanes])
            total = term if total is None else total + term
        return total

    def conv_t_inner(wide, kern):
        acc_t[...] = taps_t(wide, 1, 3, kern, 1)
        acc_t[first] += taps_t(wide, 2, 3, kern, 0)
        acc_t[second] += taps_t(wide, 1, 2, kern, 2)

    def conv_t_rim(wide, kern):
        acc_t[first] += taps_t(wide, 0, 1, kern, 2)
        acc_t[second] += taps_t(wide, 3, 4, kern, 0)

    def weight_grad(left_t, wide, name):
        for a in sorted({t // 3 for t in taps[name]}):
            g = dot(left_t[...], wide[(2 - a) * COLS : (2 - a) * COLS + TOK])
            for b in range(3):
                at = taps[name].index(3 * a + b) * width
                rows[name].part[:, at : at + width] = (
                    g[:, b * DIM : (b + 1) * DIM].astype(BF).reshape(NROW, width, DIM)
                )

    pl.semaphore_wait(barrier, len(friends))
    turn = [8, 7, 9, 6, 10, 5, 11, 4, 12, 3, 13, 2, 14, 1, 15]
    cot_copies = []
    for k in turn:
        there = (w.c + k) % NCOL
        cot_copies.append(
            remote(
                cot_h.at[pl.ds(there * 2, 2)],
                cot.at[pl.ds(1, 2), here],
                m["swap_ss"].at[k - 1],
                m["swap_rs"].at[k - 1],
                w.at_col(k),
            )
        )
        cot_copies[-1].start()
    own_cot = pltpu.make_async_copy(cot_h.at[mine], cot.at[pl.ds(1, 2), here], load.at[7])
    own_cot.start()

    act, hid, bh = m["act"], m["hid"], m["bh"]
    for name in ("tok", "wp", "bp"):
        loads[name].wait()
    loads["wi"].start()
    feature = (dot(m["tok"][...], m["wp"][...]) + m["bp"][...][None, :]).astype(BF)
    m["feat"][...] = feature
    act[1:3] = silu(feature.astype(F32)).astype(BF).reshape(2, COLS, DIM)
    act_halo = halo(act, 0)
    loads["wo"].start()
    for z in (zo, zi, zp):
        z.clear()
    expand(act, m["ea"], 1, False)
    expand(act, m["ea"], 2, False)

    loads["wi"].wait()
    conv_inner(m["ea"], m["wi"])
    m["act_t"][...] = act[1:3].reshape(TOK, DIM).T
    m["tok_t"][...] = m["tok"][...].T

    own_cot.wait()
    for c in cot_copies:
        c.wait_recv()
    cot_halo = halo(cot, 4)
    expand(cot, m["ec"], 1, True)
    expand(cot, m["ec"], 2, True)
    loads["wo"].wait()
    conv_t_inner(m["ec"], m["wo"])
    expand_rim(act, m["ea"], act_halo, False)
    conv_rim(m["ea"], m["wi"])
    loads["bi"].wait()
    pre = acc[...] + m["bi"][...][None, :]
    hid[1:3] = silu(pre).astype(BF).reshape(2, COLS, DIM)
    m["slope"][...] = silu_slope(pre)
    m["hid_t"][...] = hid[1:3].reshape(TOK, DIM).T
    weight_grad(m["hid_t"], m["ec"], "o1")
    o1.stage0()
    expand_rim(cot, m["ec"], cot_halo, True)
    o1.stage1()

    conv_t_rim(m["ec"], m["wo"])
    bh[1:3] = (acc_t[...] * m["slope"][...]).astype(BF).reshape(2, COLS, DIM)
    bh_halo = halo(bh, 6)
    weight_grad(m["hid_t"], m["ec"], "o2")
    o2.stage0()
    expand(bh, m["ea"], 1, True)
    expand(bh, m["ea"], 2, True)
    weight_grad(m["act_t"], m["ea"], "i1")
    i1.stage0()
    conv_t_inner(m["ea"], m["wi"])
    o2.stage1()
    expand_rim(bh, m["ea"], bh_halo, True)
    hid_halo = halo(hid, 2)

    weight_grad(m["act_t"], m["ea"], "i2")
    i2.stage0()
    i1.stage1()
    o1.stage2()
    conv_t_rim(m["ea"], m["wi"])
    back = acc_t[...] * silu_slope(m["feat"][...].astype(F32))
    m["bf"][...] = (cot[1:3].reshape(TOK, DIM).astype(F32) + back).astype(BF)
    pp.part[...] = dot(m["tok_t"][...], m["bf"][...]).astype(BF).reshape(NROW, VIT // NROW, DIM)
    pp.stage0()
    o2.stage2()
    i2.stage1()
    pp.stage1()
    o1.stage3()

    expand(hid, m["eh"], 1, False)
    expand(hid, m["eh"], 2, False)
    conv_inner(m["eh"], m["wo"])
    o1.stage4()
    expand_rim(hid, m["eh"], hid_halo, False)
    conv_rim(m["eh"], m["wo"])
    loads["bo"].wait()
    refined = m["feat"][...].astype(F32) + acc[...] + m["bo"][...][None, :]
    m["strip"][...] = refined.astype(BF).reshape(2, COLS, DIM)
    refined_copies = []
    for k in turn:
        there = (w.c + k) % NCOL
        refined_copies.append(
            remote(
                m["strip"].at[:, pl.ds(pl.multiple_of(there * TILE_COLS, TILE_COLS), TILE_COLS)],
                m["tile"].at[mine],
                m["swap_ss"].at[14 + k],
                m["swap_rs"].at[14 + k],
                w.at_col(k),
            )
        )
        refined_copies[-1].start()
    own_refined = pltpu.make_async_copy(m["strip"].at[:, here], m["tile"].at[mine], load.at[8])
    own_refined.start()
    i1.stage2()
    o2.stage3()
    m["gtok"][...] = dot_nt(m["bf"][...], m["wp"][...]).astype(BF)
    gtok_copy = pltpu.make_async_copy(m["gtok"], gtok_o, load.at[9])
    gtok_copy.start()
    i1.stage3()
    i2.stage2()
    o2.stage4()
    zo.stage4()
    i1.stage4()
    pp.stage2()
    i2.stage3()
    pp.stage3()
    i2.stage4()
    zi.stage4()
    pp.stage4()
    zp.stage4()
    zo.stage5()
    own_refined.wait()
    for c in refined_copies:
        c.wait_recv()
    refined_copy = pltpu.make_async_copy(m["tile"], refined_o, load.at[10])
    refined_copy.start()
    zi.stage5()
    zp.stage5()

    def put_taps(out, order):
        def put(k, value):
            for j, t in enumerate(order[k]):
                out[t] = value[:, j * width : (j + 1) * width] * scale

        return put

    def put_project(k, value):
        gproj_o[:, k * 96 : (k + 1) * 96] = value[:, :96] * scale

    zo.stage6(put_taps(gout_o, ((3, 4, 0, 1, 2), (5, 6, 7, 8))))
    zi.stage6(put_taps(gin_o, ((3, 0, 1, 2), (4, 5, 6, 7, 8))))
    zp.stage6(put_project)

    for c in act_halo + hid_halo + cot_halo + bh_halo + cot_copies + refined_copies:
        c.wait_send()
    for p in (o1, o2, i1, i2, pp, zo, zi, zp):
        p.finish()
    gtok_copy.wait()
    refined_copy.wait()


def hand_over(*refs):
    src, dst, via, sem = refs[:5], refs[5:10], refs[10:15], refs[15]
    part = TOK // 4
    views = [[ref.at[pl.ds(j * part, part)] for j in range(4)] for ref in (src[1], via[1], dst[1])]
    for k, group in enumerate((src, via, dst)):
        views[k] += [group[j] for j in (0, 2, 3, 4)]
    into = [pltpu.make_async_copy(views[0][k], views[1][k], sem.at[k]) for k in range(8)]
    out = [pltpu.make_async_copy(views[1][k], views[2][k], sem.at[8 + k]) for k in range(8)]
    for c in into:
        c.start()
    for k in range(8):
        into[k].wait()
        out[k].start()
    for c in out:
        c.wait()


def shards(tokens, wp, bp, wi, bi, wo, bo, cot):
    scale = 1.0 / math.sqrt(COLS * TILE_ROWS * NROW)
    table = scratch_table()
    hbm = pl.BlockSpec(memory_space=pl.ANY)
    vmem = pl.BlockSpec(memory_space=pltpu.VMEM)
    share, width = DIM // NCOL, DIM // NROW

    def body(*refs):
        kernel(list(table), scale, *refs)

    shapes = (
        jax.ShapeDtypeStruct((TILE_ROWS, TILE_COLS, DIM), BF),
        jax.ShapeDtypeStruct((TOK, VIT), BF),
        jax.ShapeDtypeStruct((share, VIT // NROW), F32),
        jax.ShapeDtypeStruct((9, share, width), F32),
        jax.ShapeDtypeStruct((9, share, width), F32),
    )
    results = pl.pallas_call(
        body,
        out_shape=shapes,
        in_specs=[hbm] * 8,
        out_specs=(hbm, hbm, vmem, vmem, vmem),
        scratch_shapes=list(table.values()),
        compiler_params=pltpu.CompilerParams(
            collective_id=0, has_side_effects=True, vmem_limit_bytes=60 * 1024 * 1024
        ),
        name="refine_unit",
    )(tokens, wp, bp, wi.reshape(3, WIDE, DIM), bi, wo.reshape(3, WIDE, DIM), bo, cot)
    refined, gtok, gproj, gin, gout = pl.pallas_call(
        hand_over,
        out_shape=shapes,
        in_specs=[hbm] * 5,
        out_specs=(hbm,) * 5,
        scratch_shapes=[pltpu.VMEM(v.shape, v.dtype) for v in shapes] + [pltpu.SemaphoreType.DMA((16,))],
        name="hand_over",
    )(*results)
    turn = lambda g: g.reshape(3, 3, share, width).transpose(0, 1, 3, 2)
    return refined, gtok, gproj.T, turn(gin), turn(gout)


def solution(mesh):
    in_specs = (
        P(("frame", "row", "col"), None),
        P(),
        P(),
        P(),
        P(),
        P(),
        P(),
        P(("frame", "row"), "col", None),
    )
    out_specs = (
        P(("frame", "row"), "col", None),
        P(("frame", "row", "col"), None),
        P(("frame", "row"), "col"),
        P("frame", None, "row", "col"),
        P("frame", None, "row", "col"),
    )
    return jax.shard_map(shards, mesh=mesh, in_specs=in_specs, out_specs=out_specs, check_vma=False)
```
